32 devices in a mesh: groups: 2 (over y), tok: 2 (over core), feat: 8 (over z, x).
Axes of the slice: x: 2, y: 2, z: 4, core: 2. Of those that a mesh axis runs over, the one named last changes fastest.
Arguments:
- inputs: bfloat16 [3, 512, 3584], P(None, ('groups', 'tok')), parts along dimension 1, may hold values from -6 to 6
- enc_weight: bfloat16 [3584, 16384], P('tok', 'feat'), may hold values from -0.09375 to 0.09375
- enc_bias: float32 [16384], P('feat'), may hold values from -0.6 to 0.2
- owner: int32 [536], P('feat'), may hold values from 0 to 528, as said below
Outputs:
- cooccurrence: bfloat16 [512, 1072, 512], P('tok', ('groups', 'feat')), parts along dimension 1
The draws below stay inside these ranges and needn't reach their ends.
There are 2 independent parts, one for each index of `groups`. The reference program is written for one: setup_inputs(seed, part) draws one part's arguments, and reference() takes and returns one part's arrays. A program takes and returns all parts, laid end to end along the dimension named above; an argument that names none is the same for every part. Nothing has to cross between parts.
Inputs may be any that keep to these rules, and one draw needn't show every extreme that they name: `owner`: every tile number below 528 is held by exactly one slot; the value 528 marks an empty slot, and only the last of the 67 slots of one index of feat can be empty.
All inputs are finite; a program needn't handle non-finite values.
Results may differ from the reference program's by a relative error of at most 0.007.
Values may be sent and summed in bfloat16 or wider, within the bound.
No kernel may reach another device: no remote copies, remote signals or barrier semaphores. Data moves between devices by JAX's collectives and lax.ppermute only.
A program may use at most 448 MiB of HBM per device.

```python
import jax
import jax.numpy as jnp
import numpy as np
from jax import lax

D = 3584
F = 16384
TILE = 512
MB = 3
TOK_DEV = 128
TOKENS = 256
TILES = 528
SLOTS = 67
N_TOK = 2
N_FEAT = 8


def draw_owner(key, part):
    key = jax.random.fold_in(key, 11)
    key_tiles, key_last = jax.random.split(key)
    order = jax.random.permutation(key_tiles, TILES).astype(jnp.int32)
    filled = N_FEAT * (SLOTS - 1)
    front = order[:filled].reshape(N_FEAT, SLOTS - 1)
    leftover = jnp.concatenate([order[filled:], jnp.full((N_FEAT * SLOTS - TILES,), TILES, jnp.int32)])
    last_col = jax.random.permutation(key_last, leftover).astype(jnp.int32)
    table = jnp.concatenate([front, last_col[:, None]], axis=1)
    return table.reshape(N_FEAT * SLOTS).astype(jnp.int32)


def levels(stream_key, extent, cuts, least, high):
    factor_of, own = 1.0, jax.random.fold_in(stream_key, 6)
    for position, shards_of in cuts:
        steps = jnp.exp(jax.random.uniform(jax.random.fold_in(own, position), (shards_of,), jnp.float32, least / len(cuts), high / len(cuts)))
        factor_of = factor_of * jnp.repeat(steps, extent[position] // shards_of).reshape([-1 if axis == position else 1 for axis in range(len(extent))])
    return factor_of


def centred(own_key, dims, scale, limit, cuts=(), kind=jnp.bfloat16):
    level = levels(own_key, dims, cuts, -0.22, 0.18) if cuts else 1.0
    drawn = jax.random.normal(own_key, dims, jnp.float32) * scale * level
    return jnp.minimum(jnp.maximum(drawn, -limit), limit).astype(kind)


def setup_inputs(seed: int = 0, part: int = 0) -> dict:
    streams_of = jax.random.split(jax.random.key(seed), 5)
    own_keys = jax.random.split(jax.random.fold_in(streams_of[4], part), 5)
    return {
        "inputs": centred(own_keys[0], (MB, TOKENS, D), 1.0, 6.0, ((1, 2),)),
        "enc_weight": centred(streams_of[1], (D, F), D ** -0.5, 0.09375, ((0, 2), (1, 8))),
        "enc_bias": jnp.clip(-0.6 + 0.8 * jax.random.uniform(streams_of[2], (F,), jnp.float32) ** levels(streams_of[2], (F,), ((0, 8),), -0.2, 0.2), -0.6, 0.2),
        "owner": draw_owner(jax.random.fold_in(streams_of[4], 71), part),
    }


def tile_tables(block_count):
    row_list = []
    col_list = []
    for row_block in range(block_count):
        for col_block in range(row_block, block_count):
            row_list.append(row_block)
            col_list.append(col_block)
    row_list.append(0)
    col_list.append(0)
    return np.array(row_list, np.int32), np.array(col_list, np.int32)


def reference(inputs, enc_weight, enc_bias, owner):
    flat_rows = inputs.reshape(MB * TOKENS, D)
    preact = jnp.dot(flat_rows, enc_weight, preferred_element_type=jnp.float32)
    code_rows = jnp.maximum(preact + enc_bias[None, :], 0.0).astype(jnp.bfloat16)
    shards = code_rows.reshape(MB, N_TOK, TOK_DEV, F).transpose(1, 0, 2, 3).reshape(N_TOK, MB * TOK_DEV, F)
    row_table, col_table = tile_tables(F // TILE)
    row_ids = jnp.asarray(row_table)[owner].astype(jnp.int32)
    col_ids = jnp.asarray(col_table)[owner].astype(jnp.int32)
    slot_scale = (owner < TILES).astype(jnp.float32) / (MB * TOKENS)

    def one_slot(packed):
        row_block, col_block, scale_one = packed
        summed = jnp.zeros((TILE, TILE), jnp.float32)
        for shard_idx in range(N_TOK):
            shard = shards[shard_idx]
            rows_blk = lax.dynamic_slice_in_dim(shard, row_block * TILE, TILE, 1)
            cols_blk = lax.dynamic_slice_in_dim(shard, col_block * TILE, TILE, 1)
            term = jnp.dot(rows_blk.T, cols_blk, preferred_element_type=jnp.float32) * scale_one
            term = lax.optimization_barrier(term.astype(jnp.bfloat16))
            summed = summed + term.astype(jnp.float32)
        return summed.astype(jnp.bfloat16)

    tiles = lax.map(one_slot, (row_ids, col_ids, slot_scale))
    return tiles.transpose(1, 0, 2)
```

```python
import functools

import jax
import jax.numpy as jnp
import numpy as np
from jax import lax
from jax.experimental import pallas as pl
from jax.experimental.pallas import tpu as pltpu
from jax.sharding import PartitionSpec as P

F = 16384
TILE = 512


def tile_tables(block_count):
    row_list = []
    col_list = []
    for row_block in range(block_count):
        for col_block in range(row_block, block_count):
            row_list.append(row_block)
            col_list.append(col_block)
    row_list.append(0)
    col_list.append(0)
    return (np.array(row_list, np.int32), np.array(col_list, np.int32))


def block_ids(table, tile_total, row_table, col_table):
    matches = table[:, None] == jnp.arange(tile_total + 1, dtype=jnp.int32)[None, :]
    row_ids = jnp.sum(jnp.where(matches, jnp.asarray(row_table)[None, :], 0), axis=1).astype(
        jnp.int32
    )
    col_ids = jnp.sum(jnp.where(matches, jnp.asarray(col_table)[None, :], 0), axis=1).astype(
        jnp.int32
    )
    return (row_ids, col_ids)


def slot_tables(owner, tokens):
    block_count = F // TILE
    tile_total = block_count * (block_count + 1) // 2
    row_table, col_table = tile_tables(block_count)
    row_ids, col_ids = block_ids(owner, tile_total, row_table, col_table)
    slot_scale = (owner < tile_total).astype(jnp.float32) / tokens
    return row_ids, col_ids, slot_scale


def tiles_kernel(count, held, stage, where_ref, order_ref, bound_ref, row_ref, col_ref, scale_ref, *refs):
    pieces = refs[:count]
    out_ref, codes, done_ref, stop_buf, row_buf, col_buf, out_buf = refs[count + held : -3]
    in_sem, load_sem, out_sem = refs[-3:]
    depth, _, tokens, rows = row_buf.shape
    first = bound_ref[stage]
    last = bound_ref[stage + 1]
    my_row = lax.axis_index("tok") * rows

    arrivals = [
        pltpu.make_async_copy(piece, stop_buf.at[idx], in_sem.at[idx, 0])
        for idx, piece in enumerate(pieces)
    ]
    placed = [
        pltpu.make_async_copy(
            stop_buf.at[idx], codes.at[where_ref[idx // 2], idx % 2], in_sem.at[idx, 1]
        )
        for idx in range(count)
    ]
    for c in arrivals:
        c.start()
    for c, p in zip(arrivals, placed):
        c.wait()
        p.start()
    for p in placed:
        p.wait()

    def loads(t, buf):
        slot = order_ref[t]
        row_blk = row_ref[slot]
        col_blk = col_ref[slot]
        row_at = pl.multiple_of((row_blk & 1) * TILE + my_row, rows)
        col_at = pl.multiple_of((col_blk & 1) * TILE, TILE)
        return (
            pltpu.make_async_copy(
                codes.at[row_blk >> 1, :, :, pl.ds(row_at, rows)], row_buf.at[buf], load_sem.at[buf, 0]
            ),
            pltpu.make_async_copy(
                codes.at[col_blk >> 1, :, :, pl.ds(col_at, TILE)], col_buf.at[buf], load_sem.at[buf, 1]
            ),
        )

    def store(t, buf):
        return pltpu.make_async_copy(out_buf.at[buf], out_ref.at[order_ref[t]], out_sem.at[buf])

    def ahead(t):
        @pl.when(t < last)
        def _():
            for c in loads(t, lax.rem(t, depth)):
                c.start()

    for k in range(depth - 1):
        ahead(first + k)

    def one(t, carry):
        buf = lax.rem(t, depth)
        flip = lax.rem(t, 2)
        ahead(t + depth - 1)
        for c in loads(t, buf):
            c.wait()

        @pl.when(t - first >= 2)
        def _():
            store(t - 2, flip).wait()

        tile = lax.dot_general(
            row_buf[buf].reshape(2 * tokens, rows),
            col_buf[buf].reshape(2 * tokens, TILE),
            (((0,), (0,)), ((), ())),
            preferred_element_type=jnp.float32,
        )
        out_buf[flip] = (tile * scale_ref[order_ref[t]]).astype(out_buf.dtype)
        store(t, flip).start()
        return carry

    lax.fori_loop(first, last, one, 0)
    done_ref[0] = last
    for back in (2, 1):

        @pl.when(last - first >= back)
        def _():
            store(last - back, lax.rem(last - back, 2)).wait()


def tiles(stage, kept, state, shapes, where, tables):
    pieces = [piece for entry in kept for piece in entry[:2]]
    out, codes = shapes
    _, _, tokens, _ = codes.shape
    slots, rows, _ = out.shape
    depth = 6
    smem = pl.BlockSpec(memory_space=pltpu.SMEM)
    anywhere = pl.BlockSpec(memory_space=pl.ANY)
    lead = 1 + len(tables) + len(pieces)
    return pl.pallas_call(
        functools.partial(tiles_kernel, len(pieces), len(state), stage),
        out_shape=[out, codes, jax.ShapeDtypeStruct((1,), jnp.int32)],
        in_specs=[smem] * (1 + len(tables)) + [anywhere] * (len(pieces) + len(state)),
        out_specs=[anywhere, anywhere, smem],
        input_output_aliases={lead + k: k for k in range(len(state))},
        scratch_shapes=[
            pltpu.VMEM((len(pieces), *pieces[0].shape), codes.dtype),
            pltpu.VMEM((depth, 2, tokens, rows), codes.dtype),
            pltpu.VMEM((depth, 2, tokens, TILE), codes.dtype),
            pltpu.VMEM((2, rows, TILE), out.dtype),
            pltpu.SemaphoreType.DMA((len(pieces), 2)),
            pltpu.SemaphoreType.DMA((depth, 2)),
            pltpu.SemaphoreType.DMA((2,)),
        ],
        compiler_params=pltpu.CompilerParams(vmem_limit_bytes=56 * 1024 * 1024),
        cost_estimate=pl.CostEstimate(
            flops=slots * rows * TILE * 2 * tokens // 5,
            bytes_accessed=slots * (rows + TILE) * tokens // 5,
            transcendentals=0,
        ),
    )(where, *tables, *pieces, *state)


def stage_tables(row_ids, col_ids, half_stage):
    slots = row_ids.shape[0]
    width = half_stage.shape[0]
    pick = lambda ids: jnp.sum(
        jnp.where((ids >> 1)[:, None] == jnp.arange(width)[None, :], half_stage[None, :], 0), axis=1
    )
    stage = jnp.maximum(pick(row_ids), pick(col_ids))
    idx = jnp.arange(slots, dtype=jnp.int32)
    key = stage * slots + idx
    rank = jnp.sum((key[None, :] < key[:, None]).astype(jnp.int32), axis=1)
    order = jnp.sum(jnp.where(rank[None, :] == idx[:, None], idx[None, :], 0), axis=1)
    bounds = jnp.sum(
        (stage[None, :] < jnp.arange(8, dtype=jnp.int32)[:, None]).astype(jnp.int32), axis=1
    )
    return order.astype(jnp.int32), bounds.astype(jnp.int32)


def dev(z, x):
    return z * 2 + x


def z_pairs(moves):
    return [(dev(s, x), dev(d, x)) for s, d in moves for x in range(2)]


SWAP = [(0, 1), (1, 0)]
ACROSS = [(dev(z, x), dev(z, 1 - x)) for z in range(4) for x in range(2)]
NEXT = z_pairs([(0, 1), (1, 0), (2, 3), (3, 2)])
SECOND = z_pairs([(0, 2), (2, 0), (1, 3), (3, 1)])
MIDDLE = z_pairs([(1, 2), (2, 1)])
OUTWARD = z_pairs([(1, 0), (2, 3)])

STAGES = (
    ((0, 0, 0), (0, 0, 1), (0, 1, 0), (0, 1, 1), (1, 0, 0), (2, 0, 0)),
    ((1, 1, 0), (2, 1, 0), (2, 0, 1)),
    ((2, 1, 1), (3, 0, 0)),
    ((3, 1, 0), (3, 0, 1), (1, 0, 1)),
    ((3, 1, 1), (1, 1, 1)),
)


class Mover:
    def __init__(self):
        self.seen = ()
        self.pieces = {}

    def after(self, *arrays):
        self.seen = self.seen + arrays

    def send(self, array, pairs, axis="feat"):
        if self.seen:
            array = lax.optimization_barrier((array,) + self.seen)[0]
        return lax.ppermute(array, axis, pairs)

    def keep(self, key, array):
        self.pieces[key] = (array, self.send(array, SWAP, "tok"))
        return self.pieces[key][1]


def half_at(me, key):
    z, x, half = key
    return (me ^ (2 * z + x)) * 2 + half


def gather_and_tile(a, b, row_ids, col_ids, slot_scale):
    me = lax.axis_index("feat")
    half_index = jnp.arange(2 * lax.axis_size("feat"), dtype=jnp.int32)
    half_stage = sum(
        jnp.where(half_index == half_at(me, key), stage, 0)
        for stage, keys in enumerate(STAGES)
        for key in keys
    )
    order, bounds = stage_tables(row_ids, col_ids, half_stage)
    tables = (order, bounds, row_ids, col_ids, slot_scale)
    tokens, width = a.shape
    shapes = (
        jax.ShapeDtypeStruct((row_ids.shape[0], TILE // lax.axis_size("tok"), TILE), a.dtype),
        jax.ShapeDtypeStruct((half_index.shape[0], 2, tokens, width), a.dtype),
    )
    m = Mover()

    def work(stage, state):
        keys = STAGES[stage]
        where = jnp.stack([half_at(me, key) for key in keys]).astype(jnp.int32)
        kept = [m.pieces[key] for key in keys]
        *state, done = tiles(stage, kept, state, shapes, where, tables)
        m.after(done)
        return state

    x0a = m.send(a, ACROSS)
    n1a = m.send(a, NEXT)
    n2a = m.send(a, SECOND)
    x0b = m.send(b, ACROSS)
    m.keep((0, 0, 0), a)
    m.keep((0, 0, 1), b)

    m.after(x0a, x0b, n1a, n2a)
    x1a = m.send(n1a, ACROSS)
    x2a = m.send(n2a, ACROSS)
    n2b = m.send(b, SECOND)
    fa = m.send(n2a, OUTWARD)
    m.keep((0, 1, 0), x0a)
    m.keep((0, 1, 1), x0b)
    m.keep((1, 0, 0), n1a)
    m.keep((2, 0, 0), n2a)
    state = work(0, [])

    m.after(x1a, x2a, n2b, fa)
    x2b = m.send(n2b, ACROSS)
    ga = m.send(a, MIDDLE)
    fb = m.send(n2b, OUTWARD)
    m.keep((1, 1, 0), x1a)
    m.keep((2, 1, 0), x2a)
    m.keep((2, 0, 1), n2b)
    state = work(1, state)

    m.after(x2b, ga, fb)
    n3a = fa + ga
    x3a = m.send(n3a, ACROSS)
    gb = m.send(b, MIDDLE)
    n1b = m.send(b, NEXT)
    m.keep((2, 1, 1), x2b)
    m.keep((3, 0, 0), n3a)
    state = work(2, state)

    m.after(x3a, gb, n1b)
    n3b = fb + gb
    x3b = m.send(n3b, ACROSS)
    x1b = m.send(x0b, NEXT)
    m.keep((3, 1, 0), x3a)
    m.keep((3, 0, 1), n3b)
    m.keep((1, 0, 1), n1b)
    state = work(3, state)

    m.after(x3b, x1b)
    m.keep((3, 1, 1), x3b)
    m.keep((1, 1, 1), x1b)
    return work(4, state)[0]


def encode(inputs, enc_weight, enc_bias):
    batches, tok_rows, model_width = inputs.shape
    flat = inputs.reshape(batches * tok_rows, model_width)
    depth, features = enc_weight.shape
    first = lax.axis_index("tok") == 0
    lower, upper = flat[:, :depth], flat[:, depth:]
    theirs = jnp.where(first, upper, lower)
    other = lax.ppermute(theirs, "tok", SWAP)
    mine = jnp.where(first, lower, upper)
    halves = [slice(k * features // 2, (k + 1) * features // 2) for k in range(2)]
    near = [jnp.dot(mine, enc_weight[:, cols], preferred_element_type=jnp.float32) for cols in halves]
    other = lax.optimization_barrier((other, *near))[0]
    far = []
    for cols in halves:
        if far:
            other = lax.optimization_barrier((other, part))[0]
        part = jnp.dot(other, enc_weight[:, cols], preferred_element_type=jnp.float32)
        part = part.astype(jnp.bfloat16)
        far.append(lax.ppermute(part, "tok", SWAP))
    codes = []
    for k, cols in enumerate(halves):
        if codes:
            far[k] = lax.optimization_barrier((far[k], codes[-1]))[0]
        preact = near[k] + far[k].astype(jnp.float32)
        codes.append(jnp.maximum(preact + enc_bias[None, cols], 0.0).astype(jnp.bfloat16))
    return codes


def lines_body(inputs, enc_weight, enc_bias, owner):
    batches, tok_rows, _ = inputs.shape
    tables = slot_tables(owner, batches * tok_rows * lax.axis_size("tok"))
    a, b = encode(inputs, enc_weight, enc_bias)
    return gather_and_tile(a, b, *tables).transpose(1, 0, 2)


def select_blocks(codes_batch, picker):
    block_count = picker.shape[1]
    blocks = codes_batch.reshape(
        codes_batch.shape[0], block_count, codes_batch.shape[1] // block_count
    )
    chosen = jnp.einsum("sn,knt->skt", picker, blocks, preferred_element_type=jnp.float32)
    return chosen.astype(jnp.bfloat16)


def any_body(inputs, enc_weight, enc_bias, owner):
    batches, tok_rows, model_width = inputs.shape
    flat_rows = inputs.reshape(batches * tok_rows, model_width)
    preact = jnp.dot(
        flat_rows,
        lax.all_gather(enc_weight, "tok", axis=0, tiled=True),
        preferred_element_type=jnp.float32,
    )
    code_rows = jnp.maximum(preact + enc_bias[None, :], 0.0).astype(jnp.bfloat16)
    row_ids, col_ids, slot_scale = slot_tables(owner, batches * tok_rows * lax.axis_size("tok"))
    block_range = jnp.arange(F // TILE, dtype=jnp.int32)
    row_picker = (row_ids[:, None] == block_range[None, :]).astype(jnp.bfloat16)
    col_picker = (col_ids[:, None] == block_range[None, :]).astype(jnp.bfloat16)
    gathered = lax.all_gather(code_rows, "feat", axis=1, tiled=True)
    rows_blk = select_blocks(gathered, row_picker)
    cols_blk = select_blocks(gathered, col_picker)
    product = jnp.einsum("ska,skb->asb", rows_blk, cols_blk, preferred_element_type=jnp.float32)
    running = product * slot_scale[None, :, None]
    return lax.psum_scatter(running.astype(jnp.bfloat16), "tok", scatter_dimension=0, tiled=True)


def solution(mesh):
    in_specs = (P(None, ("groups", "tok"), None), P("tok", "feat"), P("feat"), P("feat"))
    out_specs = P("tok", ("groups", "feat"), None)
    lines = mesh.shape["feat"] == 8 and mesh.shape["tok"] == 2
    body = lines_body if lines else any_body
    return jax.shard_map(body, mesh=mesh, in_specs=in_specs, out_specs=out_specs, check_vma=False)
```

```python
import functools

import jax
import jax.numpy as jnp
import numpy as np
from jax import lax
from jax.experimental import pallas as pl
from jax.experimental.pallas import tpu as pltpu
from jax.sharding import PartitionSpec as P

F = 16384
TILE = 512
ABREAST = 4


def tile_tables(block_count):
    row_list = []
    col_list = []
    for row_block in range(block_count):
        for col_block in range(row_block, block_count):
            row_list.append(row_block)
            col_list.append(col_block)
    row_list.append(0)
    col_list.append(0)
    return (np.array(row_list, np.int32), np.array(col_list, np.int32))


def block_ids(table, tile_total, row_table, col_table):
    matches = table[:, None] == jnp.arange(tile_total + 1, dtype=jnp.int32)[None, :]
    row_ids = jnp.sum(jnp.where(matches, jnp.asarray(row_table)[None, :], 0), axis=1).astype(
        jnp.int32
    )
    col_ids = jnp.sum(jnp.where(matches, jnp.asarray(col_table)[None, :], 0), axis=1).astype(
        jnp.int32
    )
    return (row_ids, col_ids)


def slot_tables(owner, tokens):
    block_count = F // TILE
    tile_total = block_count * (block_count + 1) // 2
    row_table, col_table = tile_tables(block_count)
    row_ids, col_ids = block_ids(owner, tile_total, row_table, col_table)
    slot_scale = (owner < tile_total).astype(jnp.float32) / tokens
    return row_ids, col_ids, slot_scale


def tiles_kernel(sources, count, held, stage, lead, final, *refs):
    where_ref, order_ref, bound_ref, row_ref, col_ref, scale_ref, age_ref, near_ref = refs[:8]
    pieces = refs[8 : 8 + count]
    out_ref, codes, done_ref, pool, out_buf, in_sem, keep_sem, load_sem, out_sem = refs[
        8 + count + held :
    ]
    rows = out_ref.shape[1]
    tokens = codes.shape[2]
    half_blocks = pieces[0].shape[1] // TILE
    fresh = len(sources) // 2 * half_blocks
    ring = pool.shape[0] - fresh
    first = bound_ref[stage]
    last = bound_ref[stage + 1]
    my_row = pl.multiple_of(lax.axis_index("tok") * rows, rows)

    arrivals, keeps = [], []
    for idx, (source, row) in enumerate(sources):
        for k in range(half_blocks):
            piece = pieces[source].at[pl.ds(row * tokens, tokens), pl.ds(k * TILE, TILE)]
            here = pool.at[idx // 2 * half_blocks + k, idx % 2]
            there = codes.at[where_ref[lead + idx // 2] * half_blocks + k, idx % 2]
            arrivals.append(pltpu.make_async_copy(piece, here, in_sem.at[idx, k]))
            if not final:
                keeps.append(pltpu.make_async_copy(here, there, keep_sem.at[idx, k]))
    for c in arrivals:
        c.start()

    def slot_of(t):
        return lax.rem(t - first, ring)

    def load(t, go):
        slot = order_ref[jnp.minimum(t, order_ref.shape[0] - 1)]
        row_blk = row_ref[slot]
        col_blk = col_ref[slot]
        buf = slot_of(t)

        @pl.when((t < last) & (age_ref[row_blk] != stage))
        def _():
            go(
                pltpu.make_async_copy(
                    codes.at[row_blk, :, :, pl.ds(my_row, rows)],
                    pool.at[fresh + buf, :, :, pl.ds(my_row, rows)],
                    load_sem.at[buf],
                )
            )

        @pl.when((t < last) & (age_ref[col_blk] != stage))
        def _():
            go(pltpu.make_async_copy(codes.at[col_blk], pool.at[fresh + buf], load_sem.at[buf]))

    def store(t, buf, go):
        @pl.when(t < last)
        def _():
            go(pltpu.make_async_copy(out_buf.at[buf], out_ref.at[order_ref[t]], out_sem.at[buf]))

    start = lambda c: c.start()
    wait = lambda c: c.wait()
    for k in range(2 * ABREAST):
        load(first + k, start)
    for c in arrivals:
        c.wait()
    for c in keeps:
        c.start()

    def operands(t):
        slot = order_ref[jnp.minimum(t, last - 1)]
        row_blk = row_ref[slot]
        col_blk = col_ref[slot]
        loaded = fresh + slot_of(t)
        row_at = jnp.where(age_ref[row_blk] == stage, near_ref[row_blk], loaded)
        col_at = jnp.where(age_ref[col_blk] == stage, near_ref[col_blk], loaded)
        return row_at, col_at, scale_ref[slot]

    def some(g, carry):
        t0 = first + g * ABREAST
        side = lax.rem(g, 2) * ABREAST
        for u in range(ABREAST):
            load(t0 + 2 * ABREAST + u, start)
        for u in range(ABREAST):
            load(t0 + u, wait)

        @pl.when(g >= 2)
        def _():
            for u in range(ABREAST):
                store(t0 - 2 * ABREAST + u, side + u, wait)

        for u in range(ABREAST):
            row_at, col_at, scale = operands(t0 + u)
            tile = lax.dot_general(
                pool[row_at, :, :, pl.ds(my_row, rows)].reshape(2 * tokens, rows),
                pool[col_at].reshape(2 * tokens, TILE),
                (((0,), (0,)), ((), ())),
                preferred_element_type=jnp.float32,
            )
            out_buf[side + u] = (tile * scale).astype(out_buf.dtype)
        for u in range(ABREAST):
            store(t0 + u, side + u, start)
        return carry

    groups = lax.div(last - first + ABREAST - 1, ABREAST)
    lax.fori_loop(0, groups, some, 0)
    done_ref[0] = last
    for back in (2, 1):

        @pl.when(groups >= back)
        def _():
            for u in range(ABREAST):
                g = groups - back
                store(first + g * ABREAST + u, lax.rem(g, 2) * ABREAST + u, wait)

    for c in keeps:
        c.wait()


def tiles(stage, lead, final, kept, state, shapes, tables):
    pieces, sources = [], []
    for own, far, row in kept:
        for array, at in ((own, 0), (far, row)):
            known = [k for k, piece in enumerate(pieces) if piece is array]
            if not known:
                pieces.append(array)
            sources.append((known[0] if known else len(pieces) - 1, at))
    out, codes = shapes
    slots, rows, _ = out.shape
    half_blocks = pieces[0].shape[1] // TILE
    smem = pl.BlockSpec(memory_space=pltpu.SMEM)
    anywhere = pl.BlockSpec(memory_space=pl.ANY)
    before = len(tables) + len(pieces)
    return pl.pallas_call(
        functools.partial(
            tiles_kernel, tuple(sources), len(pieces), len(state), stage, lead, final
        ),
        out_shape=[out, codes, jax.ShapeDtypeStruct((1,), jnp.int32)],
        in_specs=[smem] * len(tables) + [anywhere] * (len(pieces) + len(state)),
        out_specs=[anywhere, anywhere, smem],
        input_output_aliases={before + k: k for k in range(len(state))},
        scratch_shapes=[
            pltpu.VMEM((len(kept) * half_blocks + 3 * ABREAST, *codes.shape[1:]), codes.dtype),
            pltpu.VMEM((2 * ABREAST, rows, TILE), out.dtype),
            pltpu.SemaphoreType.DMA((len(sources), half_blocks)),
            pltpu.SemaphoreType.DMA((len(sources), half_blocks)),
            pltpu.SemaphoreType.DMA((3 * ABREAST,)),
            pltpu.SemaphoreType.DMA((2 * ABREAST,)),
        ],
        compiler_params=pltpu.CompilerParams(vmem_limit_bytes=32 * 1024 * 1024),
        cost_estimate=pl.CostEstimate(flops=1000, bytes_accessed=1000, transcendentals=0),
    )(*tables, *pieces, *state)


def stage_tables(row_ids, col_ids, age):
    slots = row_ids.shape[0]
    block = jnp.arange(age.shape[0], dtype=jnp.int32)[None, :]
    pick = lambda ids: jnp.sum(jnp.where(ids[:, None] == block, age[None, :], 0), axis=1)
    stage = jnp.maximum(pick(row_ids), pick(col_ids))
    idx = jnp.arange(slots, dtype=jnp.int32)
    key = stage * slots + idx
    rank = jnp.sum((key[None, :] < key[:, None]).astype(jnp.int32), axis=1)
    order = jnp.sum(jnp.where(rank[None, :] == idx[:, None], idx[None, :], 0), axis=1)
    bounds = jnp.sum(
        (stage[None, :] < jnp.arange(8, dtype=jnp.int32)[:, None]).astype(jnp.int32), axis=1
    )
    return order.astype(jnp.int32), bounds.astype(jnp.int32)


def dev(z, x):
    return z * 2 + x


def z_pairs(moves):
    return [(dev(s, x), dev(d, x)) for s, d in moves for x in range(2)]


SWAP = [(0, 1), (1, 0)]
ACROSS = [(dev(z, x), dev(z, 1 - x)) for z in range(4) for x in range(2)]
NEXT = z_pairs([(0, 1), (1, 0), (2, 3), (3, 2)])
SECOND = z_pairs([(0, 2), (2, 0), (1, 3), (3, 1)])
MIDDLE = z_pairs([(1, 2), (2, 1)])
OUTWARD = z_pairs([(1, 0), (2, 3)])

STAGES = (
    ((0, 0, 0), (0, 0, 1), (0, 1, 0), (0, 1, 1), (1, 0, 0), (2, 0, 0)),
    ((1, 1, 0), (2, 1, 0), (2, 0, 1)),
    ((2, 1, 1), (3, 0, 0)),
    ((3, 1, 0), (3, 0, 1), (1, 0, 1)),
    ((3, 1, 1), (1, 1, 1)),
)


class Mover:
    def __init__(self, base):
        self.base = base
        self.seen = ()
        self.pieces = {}

    def after(self, *arrays):
        self.seen = self.seen + arrays

    def send(self, array, pairs, axis="feat", early=0):
        if self.seen:
            array = lax.optimization_barrier((array,) + self.seen)[0]
        for _ in range(early):
            array = lax.optimization_barrier((array, self.base))[0]
        return lax.ppermute(array, axis, pairs)

    def keep(self, **arrays):
        group = tuple(arrays.values())
        joined = jnp.concatenate(group, axis=0) if len(group) > 1 else group[0]
        far = self.send(joined, SWAP, "tok")
        for row, (name, array) in enumerate(arrays.items()):
            self.pieces[tuple(map(int, name[1:]))] = (array, far, row)
        return far


def half_at(me, key):
    z, x, half = key
    return (me ^ (2 * z + x)) * 2 + half


def gather_and_tile(a, b, owner, row_ids, col_ids, slot_scale):
    me = lax.axis_index("feat")
    tokens, width = a.shape
    half_blocks = width // TILE
    block = jnp.arange(F // TILE, dtype=jnp.int32)
    age, near = jnp.zeros_like(block), jnp.zeros_like(block)
    for stage, keys in enumerate(STAGES):
        for at, key in enumerate(keys):
            mine = block // half_blocks == half_at(me, key)
            age = jnp.where(mine, stage, age)
            near = jnp.where(mine, at * half_blocks + block % half_blocks, near)
    order, bounds = stage_tables(row_ids, col_ids, age)
    where = jnp.stack([half_at(me, key) for keys in STAGES for key in keys]).astype(jnp.int32)
    tables = (where, order, bounds, row_ids, col_ids, slot_scale, age, near)
    shapes = (
        jax.ShapeDtypeStruct((row_ids.shape[0], TILE // lax.axis_size("tok"), TILE), a.dtype),
        jax.ShapeDtypeStruct((F // TILE, 2, tokens, TILE), a.dtype),
    )
    m = Mover(owner)

    def work(stage, state):
        kept = [m.pieces[key] for key in STAGES[stage]]
        lead = sum(len(keys) for keys in STAGES[:stage])
        final = stage == len(STAGES) - 1
        *state, done = tiles(stage, lead, final, kept, state, shapes, tables)
        m.after(done)
        return state

    x0a = m.send(a, ACROSS, early=1)
    n1a = m.send(a, NEXT)
    n2a = m.send(a, SECOND, early=1)
    x0b = m.send(b, ACROSS)
    ta = m.keep(p000=a)
    tb = m.keep(p001=b)

    m.after(x0a, x0b, n1a, n2a, ta, tb, *tables)
    x1a = m.send(n1a, ACROSS)
    x2a = m.send(n2a, ACROSS)
    n2b = m.send(b, SECOND)
    fa = m.send(n2a, OUTWARD)
    m.keep(p010=x0a, p011=x0b, p100=n1a, p200=n2a)
    state = work(0, [])

    m.after(x1a, x2a, n2b, fa)
    x2b = m.send(n2b, ACROSS, early=1)
    ga = m.send(a, MIDDLE, early=1)
    fb = m.send(n2b, OUTWARD, early=1)
    m.keep(p110=x1a)
    m.keep(p210=x2a)
    m.keep(p201=n2b)
    state = work(1, state)

    m.after(x2b, ga, fb)
    n3a = fa + ga
    x3a = m.send(n3a, ACROSS, early=1)
    gb = m.send(b, MIDDLE, early=1)
    n1b = m.send(b, NEXT)
    m.keep(p211=x2b)
    m.keep(p300=n3a)
    state = work(2, state)

    m.after(x3a, gb, n1b)
    n3b = fb + gb
    x3b = m.send(n3b, ACROSS, early=1)
    x1b = m.send(x0b, NEXT)
    m.keep(p310=x3a)
    m.keep(p301=n3b)
    m.keep(p101=n1b)
    state = work(3, state)

    m.after(x3b, x1b)
    m.keep(p311=x3b)
    m.keep(p111=x1b)
    return work(4, state)[0]


def encode(inputs, enc_weight, enc_bias):
    batches, tok_rows, model_width = inputs.shape
    flat = inputs.reshape(batches * tok_rows, model_width)
    depth, features = enc_weight.shape
    first = lax.axis_index("tok") == 0
    lower, upper = flat[:, :depth], flat[:, depth:]
    theirs = jnp.where(first, upper, lower)
    other = lax.ppermute(theirs, "tok", SWAP)
    mine = jnp.where(first, lower, upper)
    halves = [slice(k * features // 2, (k + 1) * features // 2) for k in range(2)]
    order = (1, 0)
    near, far, codes = {}, {}, {}
    dot = functools.partial(jnp.dot, preferred_element_type=jnp.float32)
    near[order[0]] = dot(mine, enc_weight[:, halves[order[0]]])
    other = lax.optimization_barrier((other, near[order[0]]))[0]
    for k in order:
        if far:
            other = lax.optimization_barrier((other, part))[0]
        part = dot(other, enc_weight[:, halves[k]]).astype(jnp.bfloat16)
        far[k] = lax.ppermute(part, "tok", SWAP)
    mine = lax.optimization_barrier((mine, part))[0]
    near[order[1]] = dot(mine, enc_weight[:, halves[order[1]]])
    for k in order:
        if codes:
            far[k] = lax.optimization_barrier((far[k], codes[order[0]]))[0]
        preact = near[k] + far[k].astype(jnp.float32) + enc_bias[None, halves[k]]
        codes[k] = jnp.maximum(preact, 0.0).astype(jnp.bfloat16)
    return codes[0], codes[1]


def lines_body(inputs, enc_weight, enc_bias, owner):
    batches, tok_rows, _ = inputs.shape
    tables = slot_tables(owner, batches * tok_rows * lax.axis_size("tok"))
    a, b = encode(inputs, enc_weight, enc_bias)
    return gather_and_tile(a, b, owner, *tables).transpose(1, 0, 2)


def select_blocks(codes_batch, picker):
    block_count = picker.shape[1]
    blocks = codes_batch.reshape(
        codes_batch.shape[0], block_count, codes_batch.shape[1] // block_count
    )
    chosen = jnp.einsum("sn,knt->skt", picker, blocks, preferred_element_type=jnp.float32)
    return chosen.astype(jnp.bfloat16)


def any_body(inputs, enc_weight, enc_bias, owner):
    batches, tok_rows, model_width = inputs.shape
    flat_rows = inputs.reshape(batches * tok_rows, model_width)
    preact = jnp.dot(
        flat_rows,
        lax.all_gather(enc_weight, "tok", axis=0, tiled=True),
        preferred_element_type=jnp.float32,
    )
    code_rows = jnp.maximum(preact + enc_bias[None, :], 0.0).astype(jnp.bfloat16)
    row_ids, col_ids, slot_scale = slot_tables(owner, batches * tok_rows * lax.axis_size("tok"))
    block_range = jnp.arange(F // TILE, dtype=jnp.int32)
    row_picker = (row_ids[:, None] == block_range[None, :]).astype(jnp.bfloat16)
    col_picker = (col_ids[:, None] == block_range[None, :]).astype(jnp.bfloat16)
    gathered = lax.all_gather(code_rows, "feat", axis=1, tiled=True)
    rows_blk = select_blocks(gathered, row_picker)
    cols_blk = select_blocks(gathered, col_picker)
    product = jnp.einsum("ska,skb->asb", rows_blk, cols_blk, preferred_element_type=jnp.float32)
    running = product * slot_scale[None, :, None]
    return lax.psum_scatter(running.astype(jnp.bfloat16), "tok", scatter_dimension=0, tiled=True)


def solution(mesh):
    in_specs = (P(None, ("groups", "tok"), None), P("tok", "feat"), P("feat"), P("feat"))
    out_specs = P("tok", ("groups", "feat"), None)
    lines = mesh.shape["feat"] == 8 and mesh.shape["tok"] == 2
    body = lines_body if lines else any_body
    return jax.shard_map(body, mesh=mesh, in_specs=in_specs, out_specs=out_specs, check_vma=False)
```

```python
import functools

import jax
import jax.numpy as jnp
import numpy as np
from jax import lax
from jax.experimental import pallas as pl
from jax.experimental.pallas import tpu as pltpu
from jax.sharding import PartitionSpec as P

F = 16384
TILE = 512
ABREAST = 4


def tile_tables(block_count):
    row_list = []
    col_list = []
    for row_block in range(block_count):
        for col_block in range(row_block, block_count):
            row_list.append(row_block)
            col_list.append(col_block)
    row_list.append(0)
    col_list.append(0)
    return (np.array(row_list, np.int32), np.array(col_list, np.int32))


def block_ids(table, tile_total, row_table, col_table):
    matches = table[:, None] == jnp.arange(tile_total + 1, dtype=jnp.int32)[None, :]
    row_ids = jnp.sum(jnp.where(matches, jnp.asarray(row_table)[None, :], 0), axis=1).astype(
        jnp.int32
    )
    col_ids = jnp.sum(jnp.where(matches, jnp.asarray(col_table)[None, :], 0), axis=1).astype(
        jnp.int32
    )
    return (row_ids, col_ids)


def slot_tables(owner, tokens):
    block_count = F // TILE
    tile_total = block_count * (block_count + 1) // 2
    row_table, col_table = tile_tables(block_count)
    row_ids, col_ids = block_ids(owner, tile_total, row_table, col_table)
    slot_scale = (owner < tile_total).astype(jnp.float32) / tokens
    return row_ids, col_ids, slot_scale


def tiles_kernel(sources, count, held, stage, lead, final, *refs):
    where_ref, order_ref, bound_ref, row_ref, col_ref, scale_ref, age_ref, near_ref = refs[:8]
    pieces = refs[8 : 8 + count]
    out_ref, codes, done_ref, pool, out_buf, in_sem, keep_sem, load_sem, out_sem = refs[
        8 + count + held :
    ]
    rows = out_ref.shape[1]
    tokens = codes.shape[2]
    half_blocks = pieces[0].shape[1] // TILE
    fresh = len(sources) // 2 * half_blocks
    ring = pool.shape[0] - fresh
    first = bound_ref[stage]
    last = bound_ref[stage + 1]
    my_row = pl.multiple_of(lax.axis_index("tok") * rows, rows)

    arrivals, keeps = [], []
    for idx, (source, row) in enumerate(sources):
        for k in range(half_blocks):
            piece = pieces[source].at[pl.ds(row * tokens, tokens), pl.ds(k * TILE, TILE)]
            here = pool.at[idx // 2 * half_blocks + k, idx % 2]
            there = codes.at[where_ref[lead + idx // 2] * half_blocks + k, idx % 2]
            arrivals.append(pltpu.make_async_copy(piece, here, in_sem.at[idx, k]))
            if not final:
                keeps.append(pltpu.make_async_copy(here, there, keep_sem.at[idx, k]))
    for c in arrivals:
        c.start()

    def slot_of(t):
        return lax.rem(t - first, ring)

    def load(t, go):
        slot = order_ref[jnp.minimum(t, order_ref.shape[0] - 1)]
        row_blk = row_ref[slot]
        col_blk = col_ref[slot]
        buf = slot_of(t)

        @pl.when((t < last) & (age_ref[row_blk] != stage))
        def _():
            go(
                pltpu.make_async_copy(
                    codes.at[row_blk, :, :, pl.ds(my_row, rows)],
                    pool.at[fresh + buf, :, :, pl.ds(my_row, rows)],
                    load_sem.at[buf],
                )
            )

        @pl.when((t < last) & (age_ref[col_blk] != stage))
        def _():
            go(pltpu.make_async_copy(codes.at[col_blk], pool.at[fresh + buf], load_sem.at[buf]))

    def store(t, buf, go):
        @pl.when(t < last)
        def _():
            go(pltpu.make_async_copy(out_buf.at[buf], out_ref.at[order_ref[t]], out_sem.at[buf]))

    start = lambda c: c.start()
    wait = lambda c: c.wait()
    for k in range(2 * ABREAST):
        load(first + k, start)
    for c in arrivals:
        c.wait()
    for c in keeps:
        c.start()

    def operands(t):
        slot = order_ref[jnp.minimum(t, last - 1)]
        row_blk = row_ref[slot]
        col_blk = col_ref[slot]
        loaded = fresh + slot_of(t)
        row_at = jnp.where(age_ref[row_blk] == stage, near_ref[row_blk], loaded)
        col_at = jnp.where(age_ref[col_blk] == stage, near_ref[col_blk], loaded)
        return row_at, col_at, scale_ref[slot]

    def some(g, carry):
        t0 = first + g * ABREAST
        side = lax.rem(g, 2) * ABREAST
        for u in range(ABREAST):
            load(t0 + 2 * ABREAST + u, start)
        for u in range(ABREAST):
            load(t0 + u, wait)

        @pl.when(g >= 2)
        def _():
            for u in range(ABREAST):
                store(t0 - 2 * ABREAST + u, side + u, wait)

        for u in range(ABREAST):
            row_at, col_at, scale = operands(t0 + u)
            tile = lax.dot_general(
                pool[row_at, :, :, pl.ds(my_row, rows)].reshape(2 * tokens, rows),
                pool[col_at].reshape(2 * tokens, TILE),
                (((0,), (0,)), ((), ())),
                preferred_element_type=jnp.float32,
            )
            out_buf[side + u] = (tile * scale).astype(out_buf.dtype)
        for u in range(ABREAST):
            store(t0 + u, side + u, start)
        return carry

    groups = lax.div(last - first + ABREAST - 1, ABREAST)
    lax.fori_loop(0, groups, some, 0)
    done_ref[0] = last
    for back in (2, 1):

        @pl.when(groups >= back)
        def _():
            for u in range(ABREAST):
                g = groups - back
                store(first + g * ABREAST + u, lax.rem(g, 2) * ABREAST + u, wait)

    for c in keeps:
        c.wait()


def tiles(stage, lead, final, kept, state, shapes, tables):
    pieces, sources = [], []
    for own, far, row in kept:
        for array, at in ((own, 0), (far, row)):
            known = [k for k, piece in enumerate(pieces) if piece is array]
            if not known:
                pieces.append(array)
            sources.append((known[0] if known else len(pieces) - 1, at))
    out, codes = shapes
    slots, rows, _ = out.shape
    half_blocks = pieces[0].shape[1] // TILE
    smem = pl.BlockSpec(memory_space=pltpu.SMEM)
    anywhere = pl.BlockSpec(memory_space=pl.ANY)
    before = len(tables) + len(pieces)
    return pl.pallas_call(
        functools.partial(
            tiles_kernel, tuple(sources), len(pieces), len(state), stage, lead, final
        ),
        out_shape=[out, codes, jax.ShapeDtypeStruct((1,), jnp.int32)],
        in_specs=[smem] * len(tables) + [anywhere] * (len(pieces) + len(state)),
        out_specs=[anywhere, anywhere, smem],
        input_output_aliases={before + k: k for k in range(len(state))},
        scratch_shapes=[
            pltpu.VMEM((len(kept) * half_blocks + 3 * ABREAST, *codes.shape[1:]), codes.dtype),
            pltpu.VMEM((2 * ABREAST, rows, TILE), out.dtype),
            pltpu.SemaphoreType.DMA((len(sources), half_blocks)),
            pltpu.SemaphoreType.DMA((len(sources), half_blocks)),
            pltpu.SemaphoreType.DMA((3 * ABREAST,)),
            pltpu.SemaphoreType.DMA((2 * ABREAST,)),
        ],
        compiler_params=pltpu.CompilerParams(vmem_limit_bytes=32 * 1024 * 1024),
        cost_estimate=pl.CostEstimate(flops=1000, bytes_accessed=1000, transcendentals=0),
    )(*tables, *pieces, *state)


def stage_tables(row_ids, col_ids, age):
    slots = row_ids.shape[0]
    block = jnp.arange(age.shape[0], dtype=jnp.int32)[None, :]
    pick = lambda ids: jnp.sum(jnp.where(ids[:, None] == block, age[None, :], 0), axis=1)
    stage = jnp.maximum(pick(row_ids), pick(col_ids))
    idx = jnp.arange(slots, dtype=jnp.int32)
    key = stage * slots + idx
    rank = jnp.sum((key[None, :] < key[:, None]).astype(jnp.int32), axis=1)
    order = jnp.sum(jnp.where(rank[None, :] == idx[:, None], idx[None, :], 0), axis=1)
    bounds = jnp.sum(
        (stage[None, :] < jnp.arange(8, dtype=jnp.int32)[:, None]).astype(jnp.int32), axis=1
    )
    return order.astype(jnp.int32), bounds.astype(jnp.int32)


def dev(z, x):
    return z * 2 + x


def z_pairs(moves):
    return [(dev(s, x), dev(d, x)) for s, d in moves for x in range(2)]


SWAP = [(0, 1), (1, 0)]
ACROSS = [(dev(z, x), dev(z, 1 - x)) for z in range(4) for x in range(2)]
NEXT = z_pairs([(0, 1), (1, 0), (2, 3), (3, 2)])
SECOND = z_pairs([(0, 2), (2, 0), (1, 3), (3, 1)])
MIDDLE = z_pairs([(1, 2), (2, 1)])
OUTWARD = z_pairs([(1, 0), (2, 3)])

STAGES = (
    ((0, 0, 0), (0, 0, 1), (0, 1, 0), (0, 1, 1), (1, 0, 0), (2, 0, 0)),
    ((1, 1, 0), (2, 1, 0), (2, 0, 1)),
    ((2, 1, 1), (3, 0, 0)),
    ((3, 1, 0), (3, 0, 1), (1, 0, 1)),
    ((3, 1, 1), (1, 1, 1)),
)


class Mover:
    def __init__(self, base):
        self.base = base
        self.seen = ()
        self.pieces = {}

    def after(self, *arrays):
        self.seen = self.seen + arrays

    def send(self, array, pairs, axis="feat", early=0):
        if self.seen:
            array = lax.optimization_barrier((array,) + self.seen)[0]
        for _ in range(early):
            array = lax.optimization_barrier((array, self.base))[0]
        return lax.ppermute(array, axis, pairs)

    def keep(self, **arrays):
        group = tuple(arrays.values())
        joined = jnp.concatenate(group, axis=0) if len(group) > 1 else group[0]
        far = self.send(joined, SWAP, "tok")
        for row, (name, array) in enumerate(arrays.items()):
            self.pieces[tuple(map(int, name[1:]))] = (array, far, row)
        return far


def half_at(me, key):
    z, x, half = key
    return (me ^ (2 * z + x)) * 2 + half


def gather_and_tile(a, b, owner, row_ids, col_ids, slot_scale):
    me = lax.axis_index("feat")
    tokens, width = a.shape
    half_blocks = width // TILE
    block = jnp.arange(F // TILE, dtype=jnp.int32)
    age, near = jnp.zeros_like(block), jnp.zeros_like(block)
    for stage, keys in enumerate(STAGES):
        for at, key in enumerate(keys):
            mine = block // half_blocks == half_at(me, key)
            age = jnp.where(mine, stage, age)
            near = jnp.where(mine, at * half_blocks + block % half_blocks, near)
    order, bounds = stage_tables(row_ids, col_ids, age)
    where = jnp.stack([half_at(me, key) for keys in STAGES for key in keys]).astype(jnp.int32)
    tables = (where, order, bounds, row_ids, col_ids, slot_scale, age, near)
    shapes = (
        jax.ShapeDtypeStruct((row_ids.shape[0], TILE // lax.axis_size("tok"), TILE), a.dtype),
        jax.ShapeDtypeStruct((F // TILE, 2, tokens, TILE), a.dtype),
    )
    m = Mover(owner)

    def work(stage, state):
        kept = [m.pieces[key] for key in STAGES[stage]]
        lead = sum(len(keys) for keys in STAGES[:stage])
        final = stage == len(STAGES) - 1
        *state, done = tiles(stage, lead, final, kept, state, shapes, tables)
        m.after(done)
        return state

    x0a = m.send(a, ACROSS, early=1)
    n1a = m.send(a, NEXT)
    n2a = m.send(a, SECOND, early=1)
    x0b = m.send(b, ACROSS)
    ta = m.keep(p000=a)
    tb = m.keep(p001=b)

    m.after(x0a, x0b, n1a, n2a, ta, tb, *tables)
    x1a = m.send(n1a, ACROSS)
    x2a = m.send(n2a, ACROSS)
    n2b = m.send(b, SECOND)
    fa = m.send(n2a, OUTWARD)
    m.keep(p010=x0a, p011=x0b, p100=n1a, p200=n2a)
    state = work(0, [])

    m.after(x1a, x2a, n2b, fa)
    x2b = m.send(n2b, ACROSS, early=1)
    ga = m.send(a, MIDDLE, early=1)
    fb = m.send(n2b, OUTWARD, early=1)
    m.keep(p110=x1a)
    m.keep(p210=x2a)
    m.keep(p201=n2b)
    state = work(1, state)

    m.after(x2b, ga, fb)
    n3a = fa + ga
    x3a = m.send(n3a, ACROSS, early=1)
    gb = m.send(b, MIDDLE, early=1)
    n1b = m.send(b, NEXT)
    m.keep(p211=x2b)
    m.keep(p300=n3a)
    state = work(2, state)

    m.after(x3a, gb, n1b)
    n3b = fb + gb
    x3b = m.send(n3b, ACROSS, early=1)
    x1b = m.send(x0b, NEXT)
    m.keep(p310=x3a)
    m.keep(p301=n3b)
    m.keep(p101=n1b)
    state = work(3, state)

    m.keep(p311=x3b)
    m.keep(p111=x1b)
    return work(4, state)[0]


def encode(inputs, enc_weight, enc_bias):
    batches, tok_rows, model_width = inputs.shape
    flat = inputs.reshape(batches * tok_rows, model_width)
    depth, features = enc_weight.shape
    first = lax.axis_index("tok") == 0
    lower, upper = flat[:, :depth], flat[:, depth:]
    theirs = jnp.where(first, upper, lower)
    other = lax.ppermute(theirs, "tok", SWAP)
    mine = jnp.where(first, lower, upper)
    halves = [slice(k * features // 2, (k + 1) * features // 2) for k in range(2)]
    order = (1, 0)
    near, far, codes = {}, {}, {}
    dot = functools.partial(jnp.dot, preferred_element_type=jnp.float32)
    near[order[0]] = dot(mine, enc_weight[:, halves[order[0]]])
    other = lax.optimization_barrier((other, near[order[0]]))[0]
    for k in order:
        if far:
            other = lax.optimization_barrier((other, part))[0]
        part = dot(other, enc_weight[:, halves[k]]).astype(jnp.bfloat16)
        far[k] = lax.ppermute(part, "tok", SWAP)
    mine = lax.optimization_barrier((mine, part))[0]
    near[order[1]] = dot(mine, enc_weight[:, halves[order[1]]])
    for k in order:
        if codes:
            far[k] = lax.optimization_barrier((far[k], codes[order[0]]))[0]
        preact = near[k] + far[k].astype(jnp.float32) + enc_bias[None, halves[k]]
        codes[k] = jnp.maximum(preact, 0.0).astype(jnp.bfloat16)
    return codes[0], codes[1]


def lines_body(inputs, enc_weight, enc_bias, owner):
    batches, tok_rows, _ = inputs.shape
    tables = slot_tables(owner, batches * tok_rows * lax.axis_size("tok"))
    a, b = encode(inputs, enc_weight, enc_bias)
    return gather_and_tile(a, b, owner, *tables).transpose(1, 0, 2)


def select_blocks(codes_batch, picker):
    block_count = picker.shape[1]
    blocks = codes_batch.reshape(
        codes_batch.shape[0], block_count, codes_batch.shape[1] // block_count
    )
    chosen = jnp.einsum("sn,knt->skt", picker, blocks, preferred_element_type=jnp.float32)
    return chosen.astype(jnp.bfloat16)


def any_body(inputs, enc_weight, enc_bias, owner):
    batches, tok_rows, model_width = inputs.shape
    flat_rows = inputs.reshape(batches * tok_rows, model_width)
    preact = jnp.dot(
        flat_rows,
        lax.all_gather(enc_weight, "tok", axis=0, tiled=True),
        preferred_element_type=jnp.float32,
    )
    code_rows = jnp.maximum(preact + enc_bias[None, :], 0.0).astype(jnp.bfloat16)
    row_ids, col_ids, slot_scale = slot_tables(owner, batches * tok_rows * lax.axis_size("tok"))
    block_range = jnp.arange(F // TILE, dtype=jnp.int32)
    row_picker = (row_ids[:, None] == block_range[None, :]).astype(jnp.bfloat16)
    col_picker = (col_ids[:, None] == block_range[None, :]).astype(jnp.bfloat16)
    gathered = lax.all_gather(code_rows, "feat", axis=1, tiled=True)
    rows_blk = select_blocks(gathered, row_picker)
    cols_blk = select_blocks(gathered, col_picker)
    product = jnp.einsum("ska,skb->asb", rows_blk, cols_blk, preferred_element_type=jnp.float32)
    running = product * slot_scale[None, :, None]
    return lax.psum_scatter(running.astype(jnp.bfloat16), "tok", scatter_dimension=0, tiled=True)


def solution(mesh):
    in_specs = (P(None, ("groups", "tok"), None), P("tok", "feat"), P("feat"), P("feat"))
    out_specs = P("tok", ("groups", "feat"), None)
    lines = mesh.shape["feat"] == 8 and mesh.shape["tok"] == 2
    body = lines_body if lines else any_body
    return jax.shard_map(body, mesh=mesh, in_specs=in_specs, out_specs=out_specs, check_vma=False)
```

```python
import functools

import jax
import jax.numpy as jnp
import numpy as np
from jax import lax
from jax.experimental import pallas as pl
from jax.experimental.pallas import tpu as pltpu
from jax.sharding import PartitionSpec as P

F = 16384
TILE = 512
ABREAST = 4


def tile_tables(block_count):
    row_list = []
    col_list = []
    for row_block in range(block_count):
        for col_block in range(row_block, block_count):
            row_list.append(row_block)
            col_list.append(col_block)
    row_list.append(0)
    col_list.append(0)
    return (np.array(row_list, np.int32), np.array(col_list, np.int32))


def block_ids(table, tile_total, row_table, col_table):
    matches = table[:, None] == jnp.arange(tile_total + 1, dtype=jnp.int32)[None, :]
    row_ids = jnp.sum(jnp.where(matches, jnp.asarray(row_table)[None, :], 0), axis=1).astype(
        jnp.int32
    )
    col_ids = jnp.sum(jnp.where(matches, jnp.asarray(col_table)[None, :], 0), axis=1).astype(
        jnp.int32
    )
    return (row_ids, col_ids)


def slot_tables(owner, tokens):
    block_count = F // TILE
    tile_total = block_count * (block_count + 1) // 2
    row_table, col_table = tile_tables(block_count)
    row_ids, col_ids = block_ids(owner, tile_total, row_table, col_table)
    slot_scale = (owner < tile_total).astype(jnp.float32) / tokens
    return row_ids, col_ids, slot_scale


def tiles_kernel(sources, count, held, stage, lead, final, *refs):
    where_ref, order_ref, bound_ref, row_ref, col_ref, scale_ref, age_ref, near_ref = refs[:8]
    pieces = refs[8 : 8 + count]
    out_ref, codes, done_ref, pool, out_buf, in_sem, keep_sem, load_sem, out_sem = refs[
        8 + count + held :
    ]
    rows = out_ref.shape[1]
    tokens = codes.shape[2]
    half_blocks = pieces[0].shape[1] // TILE
    fresh = len(sources) // 2 * half_blocks
    ring = pool.shape[0] - fresh
    first = bound_ref[stage]
    last = bound_ref[stage + 1]
    my_row = pl.multiple_of(lax.axis_index("tok") * rows, rows)

    arrivals, keeps = [], []
    for idx, (source, row) in enumerate(sources):
        for k in range(half_blocks):
            piece = pieces[source].at[pl.ds(row * tokens, tokens), pl.ds(k * TILE, TILE)]
            here = pool.at[idx // 2 * half_blocks + k, idx % 2]
            there = codes.at[where_ref[lead + idx // 2] * half_blocks + k, idx % 2]
            arrivals.append(pltpu.make_async_copy(piece, here, in_sem.at[idx, k]))
            if not final:
                keeps.append(pltpu.make_async_copy(here, there, keep_sem.at[idx, k]))
    for c in arrivals:
        c.start()

    def slot_of(t):
        return lax.rem(t - first, ring)

    def load(t, go):
        slot = order_ref[jnp.minimum(t, order_ref.shape[0] - 1)]
        row_blk = row_ref[slot]
        col_blk = col_ref[slot]
        buf = slot_of(t)

        @pl.when((t < last) & (age_ref[row_blk] != stage))
        def _():
            go(
                pltpu.make_async_copy(
                    codes.at[row_blk, :, :, pl.ds(my_row, rows)],
                    pool.at[fresh + buf, :, :, pl.ds(my_row, rows)],
                    load_sem.at[buf],
                )
            )

        @pl.when((t < last) & (age_ref[col_blk] != stage))
        def _():
            go(pltpu.make_async_copy(codes.at[col_blk], pool.at[fresh + buf], load_sem.at[buf]))

    def store(t, buf, go):
        @pl.when(t < last)
        def _():
            go(pltpu.make_async_copy(out_buf.at[buf], out_ref.at[order_ref[t]], out_sem.at[buf]))

    start = lambda c: c.start()
    wait = lambda c: c.wait()
    for k in range(2 * ABREAST):
        load(first + k, start)
    for c in arrivals:
        c.wait()
    for c in keeps:
        c.start()

    def operands(t):
        slot = order_ref[jnp.minimum(t, last - 1)]
        row_blk = row_ref[slot]
        col_blk = col_ref[slot]
        loaded = fresh + slot_of(t)
        row_at = jnp.where(age_ref[row_blk] == stage, near_ref[row_blk], loaded)
        col_at = jnp.where(age_ref[col_blk] == stage, near_ref[col_blk], loaded)
        return row_at, col_at, scale_ref[slot]

    def some(g, carry):
        t0 = first + g * ABREAST
        side = lax.rem(g, 2) * ABREAST
        for u in range(ABREAST):
            load(t0 + 2 * ABREAST + u, start)
        for u in range(ABREAST):
            load(t0 + u, wait)

        @pl.when(g >= 2)
        def _():
            for u in range(ABREAST):
                store(t0 - 2 * ABREAST + u, side + u, wait)

        for u in range(ABREAST):
            row_at, col_at, scale = operands(t0 + u)
            tile = lax.dot_general(
                pool[row_at, :, :, pl.ds(my_row, rows)].reshape(2 * tokens, rows),
                pool[col_at].reshape(2 * tokens, TILE),
                (((0,), (0,)), ((), ())),
                preferred_element_type=jnp.float32,
            )
            out_buf[side + u] = (tile * scale).astype(out_buf.dtype)
        for u in range(ABREAST):
            store(t0 + u, side + u, start)
        return carry

    groups = lax.div(last - first + ABREAST - 1, ABREAST)
    lax.fori_loop(0, groups, some, 0)
    done_ref[0] = last
    for back in (2, 1):

        @pl.when(groups >= back)
        def _():
            for u in range(ABREAST):
                g = groups - back
                store(first + g * ABREAST + u, lax.rem(g, 2) * ABREAST + u, wait)

    for c in keeps:
        c.wait()


def tiles(stage, lead, final, kept, state, shapes, tables):
    pieces, sources = [], []
    for own, far, row in kept:
        for array, at in ((own, 0), (far, row)):
            known = [k for k, piece in enumerate(pieces) if piece is array]
            if not known:
                pieces.append(array)
            sources.append((known[0] if known else len(pieces) - 1, at))
    out, codes = shapes
    slots, rows, _ = out.shape
    half_blocks = pieces[0].shape[1] // TILE
    smem = pl.BlockSpec(memory_space=pltpu.SMEM)
    anywhere = pl.BlockSpec(memory_space=pl.ANY)
    before = len(tables) + len(pieces)
    return pl.pallas_call(
        functools.partial(
            tiles_kernel, tuple(sources), len(pieces), len(state), stage, lead, final
        ),
        out_shape=[out, codes, jax.ShapeDtypeStruct((1,), jnp.int32)],
        in_specs=[smem] * len(tables) + [anywhere] * (len(pieces) + len(state)),
        out_specs=[anywhere, anywhere, smem],
        input_output_aliases={before + k: k for k in range(len(state))},
        scratch_shapes=[
            pltpu.VMEM((len(kept) * half_blocks + 3 * ABREAST, *codes.shape[1:]), codes.dtype),
            pltpu.VMEM((2 * ABREAST, rows, TILE), out.dtype),
            pltpu.SemaphoreType.DMA((len(sources), half_blocks)),
            pltpu.SemaphoreType.DMA((len(sources), half_blocks)),
            pltpu.SemaphoreType.DMA((3 * ABREAST,)),
            pltpu.SemaphoreType.DMA((2 * ABREAST,)),
        ],
        compiler_params=pltpu.CompilerParams(vmem_limit_bytes=32 * 1024 * 1024),
        cost_estimate=pl.CostEstimate(flops=1000, bytes_accessed=1000, transcendentals=0),
    )(*tables, *pieces, *state)


def stage_tables(row_ids, col_ids, age):
    slots = row_ids.shape[0]
    block = jnp.arange(age.shape[0], dtype=jnp.int32)[None, :]
    pick = lambda ids: jnp.sum(jnp.where(ids[:, None] == block, age[None, :], 0), axis=1)
    stage = jnp.maximum(pick(row_ids), pick(col_ids))
    idx = jnp.arange(slots, dtype=jnp.int32)
    key = stage * slots + idx
    rank = jnp.sum((key[None, :] < key[:, None]).astype(jnp.int32), axis=1)
    order = jnp.sum(jnp.where(rank[None, :] == idx[:, None], idx[None, :], 0), axis=1)
    bounds = jnp.sum(
        (stage[None, :] < jnp.arange(8, dtype=jnp.int32)[:, None]).astype(jnp.int32), axis=1
    )
    return order.astype(jnp.int32), bounds.astype(jnp.int32)


def dev(z, x):
    return z * 2 + x


def z_pairs(moves):
    return [(dev(s, x), dev(d, x)) for s, d in moves for x in range(2)]


SWAP = [(0, 1), (1, 0)]
ACROSS = [(dev(z, x), dev(z, 1 - x)) for z in range(4) for x in range(2)]
NEXT = z_pairs([(0, 1), (1, 0), (2, 3), (3, 2)])
SECOND = z_pairs([(0, 2), (2, 0), (1, 3), (3, 1)])
MIDDLE = z_pairs([(1, 2), (2, 1)])
OUTWARD = z_pairs([(1, 0), (2, 3)])

STAGES = (
    ((0, 0, 0), (0, 0, 1), (0, 1, 0), (0, 1, 1), (1, 0, 0), (2, 0, 0)),
    ((1, 1, 0), (2, 1, 0), (2, 0, 1)),
    ((2, 1, 1), (3, 0, 0)),
    ((3, 1, 0), (3, 0, 1), (1, 0, 1)),
    ((3, 1, 1), (1, 1, 1)),
)


class Mover:
    def __init__(self, base):
        self.base = base
        self.seen = ()
        self.pieces = {}

    def after(self, *arrays):
        self.seen = self.seen + arrays

    def send(self, array, pairs, axis="feat", early=0):
        if self.seen:
            array = lax.optimization_barrier((array,) + self.seen)[0]
        for _ in range(early):
            array = lax.optimization_barrier((array, self.base))[0]
        return lax.ppermute(array, axis, pairs)

    def keep(self, **arrays):
        group = tuple(arrays.values())
        joined = jnp.concatenate(group, axis=0) if len(group) > 1 else group[0]
        far = self.send(joined, SWAP, "tok")
        for row, (name, array) in enumerate(arrays.items()):
            self.pieces[tuple(map(int, name[1:]))] = (array, far, row)
        return far


def half_at(me, key):
    z, x, half = key
    return (me ^ (2 * z + x)) * 2 + half


def gather_and_tile(a, b, owner, row_ids, col_ids, slot_scale):
    me = lax.axis_index("feat")
    tokens, width = a.shape
    half_blocks = width // TILE
    block = jnp.arange(F // TILE, dtype=jnp.int32)
    age, near = jnp.zeros_like(block), jnp.zeros_like(block)
    for stage, keys in enumerate(STAGES):
        for at, key in enumerate(keys):
            mine = block // half_blocks == half_at(me, key)
            age = jnp.where(mine, stage, age)
            near = jnp.where(mine, at * half_blocks + block % half_blocks, near)
    order, bounds = stage_tables(row_ids, col_ids, age)
    where = jnp.stack([half_at(me, key) for keys in STAGES for key in keys]).astype(jnp.int32)
    tables = (where, order, bounds, row_ids, col_ids, slot_scale, age, near)
    shapes = (
        jax.ShapeDtypeStruct((row_ids.shape[0], TILE // lax.axis_size("tok"), TILE), a.dtype),
        jax.ShapeDtypeStruct((F // TILE, 2, tokens, TILE), a.dtype),
    )
    m = Mover(owner)

    def work(stage, state):
        kept = [m.pieces[key] for key in STAGES[stage]]
        lead = sum(len(keys) for keys in STAGES[:stage])
        final = stage == len(STAGES) - 1
        *state, done = tiles(stage, lead, final, kept, state, shapes, tables)
        m.after(done)
        return state

    x0a = m.send(a, ACROSS, early=1)
    n1a = m.send(a, NEXT)
    n2a = m.send(a, SECOND, early=1)
    x0b = m.send(b, ACROSS)
    ta = m.keep(p000=a)
    tb = m.keep(p001=b)

    m.after(x0a, x0b, n1a, n2a, ta, tb, *tables)
    x1a = m.send(n1a, ACROSS)
    x2a = m.send(n2a, ACROSS)
    n2b = m.send(b, SECOND)
    fa = m.send(n2a, OUTWARD)
    m.keep(p010=x0a, p011=x0b, p100=n1a, p200=n2a)
    state = work(0, [])

    m.after(x1a, x2a, n2b, fa)
    x2b = m.send(n2b, ACROSS, early=1)
    ga = m.send(a, MIDDLE, early=1)
    fb = m.send(n2b, OUTWARD, early=1)
    m.keep(p110=x1a)
    m.keep(p210=x2a)
    m.keep(p201=n2b)
    state = work(1, state)

    m.after(x2b, ga, fb)
    n3a = fa + ga
    x3a = m.send(n3a, ACROSS, early=1)
    gb = m.send(b, MIDDLE, early=1)
    n1b = m.send(b, NEXT)
    m.keep(p211=x2b)
    m.keep(p300=n3a)
    state = work(2, state)

    m.after(x3a, gb)
    n3b = fb + gb
    x3b = m.send(n3b, ACROSS, early=1)
    x1b = m.send(x0b, NEXT)
    m.keep(p310=x3a)
    m.keep(p301=n3b)
    m.keep(p101=n1b)
    state = work(3, state)

    m.keep(p311=x3b)
    m.keep(p111=x1b)
    return work(4, state)[0]


def encode(inputs, enc_weight, enc_bias):
    batches, tok_rows, model_width = inputs.shape
    flat = inputs.reshape(batches * tok_rows, model_width)
    depth, features = enc_weight.shape
    first = lax.axis_index("tok") == 0
    lower, upper = flat[:, :depth], flat[:, depth:]
    theirs = jnp.where(first, upper, lower)
    other = lax.ppermute(theirs, "tok", SWAP)
    mine = jnp.where(first, lower, upper)
    halves = [slice(k * features // 2, (k + 1) * features // 2) for k in range(2)]
    order = (1, 0)
    near, far, codes = {}, {}, {}
    dot = functools.partial(jnp.dot, preferred_element_type=jnp.float32)
    near[order[0]] = dot(mine, enc_weight[:, halves[order[0]]])
    other = lax.optimization_barrier((other, near[order[0]]))[0]
    for k in order:
        if far:
            other = lax.optimization_barrier((other, part))[0]
        part = dot(other, enc_weight[:, halves[k]]).astype(jnp.bfloat16)
        far[k] = lax.ppermute(part, "tok", SWAP)
    mine = lax.optimization_barrier((mine, part))[0]
    near[order[1]] = dot(mine, enc_weight[:, halves[order[1]]])
    for k in order:
        if codes:
            far[k] = lax.optimization_barrier((far[k], codes[order[0]]))[0]
        preact = near[k] + far[k].astype(jnp.float32) + enc_bias[None, halves[k]]
        codes[k] = jnp.maximum(preact, 0.0).astype(jnp.bfloat16)
    return codes[0], codes[1]


def lines_body(inputs, enc_weight, enc_bias, owner):
    batches, tok_rows, _ = inputs.shape
    tables = slot_tables(owner, batches * tok_rows * lax.axis_size("tok"))
    a, b = encode(inputs, enc_weight, enc_bias)
    return gather_and_tile(a, b, owner, *tables).transpose(1, 0, 2)


def select_blocks(codes_batch, picker):
    block_count = picker.shape[1]
    blocks = codes_batch.reshape(
        codes_batch.shape[0], block_count, codes_batch.shape[1] // block_count
    )
    chosen = jnp.einsum("sn,knt->skt", picker, blocks, preferred_element_type=jnp.float32)
    return chosen.astype(jnp.bfloat16)


def any_body(inputs, enc_weight, enc_bias, owner):
    batches, tok_rows, model_width = inputs.shape
    flat_rows = inputs.reshape(batches * tok_rows, model_width)
    preact = jnp.dot(
        flat_rows,
        lax.all_gather(enc_weight, "tok", axis=0, tiled=True),
        preferred_element_type=jnp.float32,
    )
    code_rows = jnp.maximum(preact + enc_bias[None, :], 0.0).astype(jnp.bfloat16)
    row_ids, col_ids, slot_scale = slot_tables(owner, batches * tok_rows * lax.axis_size("tok"))
    block_range = jnp.arange(F // TILE, dtype=jnp.int32)
    row_picker = (row_ids[:, None] == block_range[None, :]).astype(jnp.bfloat16)
    col_picker = (col_ids[:, None] == block_range[None, :]).astype(jnp.bfloat16)
    gathered = lax.all_gather(code_rows, "feat", axis=1, tiled=True)
    rows_blk = select_blocks(gathered, row_picker)
    cols_blk = select_blocks(gathered, col_picker)
    product = jnp.einsum("ska,skb->asb", rows_blk, cols_blk, preferred_element_type=jnp.float32)
    running = product * slot_scale[None, :, None]
    return lax.psum_scatter(running.astype(jnp.bfloat16), "tok", scatter_dimension=0, tiled=True)


def solution(mesh):
    in_specs = (P(None, ("groups", "tok"), None), P("tok", "feat"), P("feat"), P("feat"))
    out_specs = P("tok", ("groups", "feat"), None)
    lines = mesh.shape["feat"] == 8 and mesh.shape["tok"] == 2
    body = lines_body if lines else any_body
    return jax.shard_map(body, mesh=mesh, in_specs=in_specs, out_specs=out_specs, check_vma=False)
```
